512 devices in a mesh: section: 8 (over x, y_lo), ctx: 64 (over y_hi, z, core).
Axes of the slice: x: 4, y: 4 (y_hi: 2, y_lo: 2; y = y_hi * 2 + y_lo), z: 16, core: 2. Of those that a mesh axis runs over, the one named last changes fastest.
Arguments:
- queries: bfloat16 [8, 8192, 3072], P('section', 'ctx'), may hold values from -6 to 6
- key_vectors: bfloat16 [8, 8192, 128], P('section', 'ctx'), may hold values from -6 to 6
- value_vectors: bfloat16 [8, 8192, 128], P('section', 'ctx'), may hold values from -6 to 6
- first_values: bfloat16 [8192, 128], P(('ctx', 'section')), may hold values from -6 to 6
- grad_out: bfloat16 [8, 8192, 3072], P('section', 'ctx'), may hold values from -6 to 6
- doc_start: int32 [8192], P('ctx'), may hold values from 0 to 8191, as said below
- mix_table: float32 [48, 256], replicated, may hold values from 0.2 to 1.2
- layer_index: int32 [8], P('section'), may hold values from 0 to 47
Outputs:
- attended: bfloat16 [8, 8192, 3072], P('section', 'ctx')
- query_grad: bfloat16 [8, 8192, 3072], P('section', 'ctx')
- key_grad: bfloat16 [8, 8192, 128], P('section', 'ctx')
- value_grad: bfloat16 [8, 8192, 128], P('section', 'ctx')
- first_grad: float32 [8192, 128], P(('ctx', 'section'))
The draws below stay inside these ranges and needn't reach their ends.
Inputs may be any that keep to these rules, and one draw needn't show every extreme that they name: doc_start never falls, equals t where a document begins at t and 0 at t = 0, and t - doc_start[t] < 512; some document is exactly 512 positions long, and a document begins at the last position.
All inputs are finite; a program needn't handle non-finite values.
Results may differ from the reference program's by a relative error of at most 0.012.
The reference program's roundings to bfloat16 on the way count: a program that leaves them out, or rounds other values in their place, can miss the bound.
Values may be sent and summed in bfloat16 or wider, within the bound.
A program may use at most 64 MiB of HBM per device.

```python
import math
import jax
import jax.numpy as jnp
from jax import lax

HEAD = 128
HEADS = 24
QF = 3072
TOK_DEV = 128
REACH = 4
LAYERS = 48
TOKENS = 8192
N_SECTION = 8
N_CTX = 64


def draw_queries(key, part):
    key = jax.random.fold_in(key, 11)
    values_drawn = jnp.clip(jax.random.normal(key, (N_SECTION, TOKENS, HEADS, HEAD), jnp.float32), -6.0, 6.0)
    return values_drawn.reshape(N_SECTION, TOKENS, QF).astype(jnp.bfloat16)


def draw_key_vectors(key, part):
    key = jax.random.fold_in(key, 13)
    values_drawn = jnp.clip(jax.random.normal(key, (N_SECTION, TOKENS, HEAD), jnp.float32), -6.0, 6.0)
    return values_drawn.astype(jnp.bfloat16)


def draw_doc_start(key, part):
    key = jax.random.fold_in(key, 5)
    short_key, long_key, coin_key, pick_key = jax.random.split(key, 4)
    longest = REACH * TOK_DEV
    shorter = jax.random.randint(short_key, (TOKENS,), 1, longest // 8 + 1)
    longer = jax.random.randint(long_key, (TOKENS,), longest // 2, longest + 1)
    coins = jax.random.randint(coin_key, (TOKENS,), 0, 2)
    lengths = jnp.where(coins == 0, shorter, longer)
    chosen = jax.random.randint(pick_key, (), 0, 2)
    lengths = jnp.where(jnp.arange(TOKENS) == chosen, longest, lengths).astype(jnp.int32)
    starts = jnp.cumsum(lengths) - lengths
    marks = jnp.zeros((TOKENS + 1,), jnp.int32).at[jnp.minimum(starts, TOKENS)].set(1)[:TOKENS]
    positions = jnp.arange(TOKENS, dtype=jnp.int32)
    marks = jnp.where(positions == TOKENS - 1, 1, marks)
    return lax.cummax(jnp.where(marks == 1, positions, 0), axis=0).astype(jnp.int32)


def with_ends(values, key, least, top_value):
    spot = [jax.random.randint(jax.random.fold_in(key, axis), (), 0, length) for axis, length in enumerate(values.shape)]
    widest = values.shape.index(max(values.shape))
    neighbour = spot[:widest] + [(spot[widest] + 1) % values.shape[widest]] + spot[widest + 1:]
    return values.at[tuple(spot)].set(least).at[tuple(neighbour)].set(top_value)


def levels(key, dims, shards, least, largest):
    factor_of, own = 1.0, jax.random.fold_in(key, 6)
    for dim, shards_of in shards:
        steps = jnp.exp(jax.random.uniform(jax.random.fold_in(own, dim), (shards_of,), jnp.float32, least / len(shards), largest / len(shards)))
        factor_of = factor_of * jnp.repeat(steps, dims[dim] // shards_of).reshape([-1 if axis == dim else 1 for axis in range(len(dims))])
    return factor_of


def scatter_about(rng, dims, spread, reach, pieces=(), kind=jnp.bfloat16):
    gain = levels(rng, dims, pieces, -0.22, 0.18) if pieces else 1.0
    array = jax.random.normal(rng, dims, jnp.float32) * spread * gain
    return jnp.minimum(jnp.maximum(array, -reach), reach).astype(kind)


def setup_inputs(seed: int = 0) -> dict:
    key_list = jax.random.split(jax.random.key(seed), 9)
    queries = draw_queries(jax.random.fold_in(key_list[8], 71), 0)
    key_vectors = draw_key_vectors(jax.random.fold_in(key_list[8], 71), 0)
    value_vectors = scatter_about(key_list[2], (N_SECTION, TOKENS, HEAD), 1.0, 6.0, ((0, 8), (1, 64)))
    first_values = scatter_about(key_list[3], (TOKENS, HEAD), 1.0, 6.0, ((0, 512),))
    grad_out = scatter_about(key_list[4], (N_SECTION, TOKENS, QF), 1.0, 6.0, ((0, 8), (1, 64)))
    doc_start = draw_doc_start(jax.random.fold_in(key_list[8], 71), 0)
    mix_table = jnp.clip(jax.random.uniform(key_list[6], (LAYERS, 2 * HEAD), jnp.float32, 0.2, 1.2), 0.2, 1.2)
    layer_index = with_ends(jax.random.randint(key_list[7], (N_SECTION,), 0, LAYERS), jax.random.fold_in(key_list[7], 1), 0, LAYERS - 1).astype(jnp.int32)
    return dict(queries=queries, key_vectors=key_vectors, value_vectors=value_vectors, first_values=first_values, grad_out=grad_out, doc_start=doc_start, mix_table=mix_table, layer_index=layer_index)


def window_pass(query_rows, grad_rows, key_window, value_window, starts, query_first, key_first, score_scale, head_count):
    row_count = query_rows.shape[0]
    head_width = key_window.shape[1]
    key_count = key_window.shape[0]
    query_flat = query_rows.reshape(row_count * head_count, head_width)
    grad_flat = grad_rows.reshape(row_count * head_count, head_width)
    key_positions = key_first + jnp.arange(key_count, dtype=jnp.int32)
    query_positions = query_first + jnp.arange(row_count, dtype=jnp.int32)
    allowed = (key_positions[None, :] >= starts[:, None]) & (key_positions[None, :] <= query_positions[:, None])
    contract_last = (((1,), (1,)), ((), ()))
    contract_first = (((0,), (0,)), ((), ()))
    scores = lax.dot_general(query_flat, key_window, contract_last, preferred_element_type=jnp.float32) * score_scale
    scores = jnp.where(allowed[:, None, :], scores.reshape(row_count, head_count, key_count), -jnp.inf)
    row_max = lax.optimization_barrier(jnp.max(scores, axis=2, keepdims=True))
    weights = jnp.exp(scores - row_max)
    weights = weights / lax.optimization_barrier(jnp.sum(weights, axis=2, keepdims=True))
    weights = weights.reshape(row_count * head_count, key_count)
    packed = weights.astype(jnp.bfloat16)
    context = jnp.dot(packed, value_window, preferred_element_type=jnp.float32)
    grad_weights = lax.dot_general(grad_flat, value_window, contract_last, preferred_element_type=jnp.float32)
    row_dot = lax.optimization_barrier(jnp.sum(grad_flat.astype(jnp.float32) * context, axis=1, keepdims=True))
    grad_scores = (weights * (grad_weights - row_dot)).astype(jnp.bfloat16)
    query_grad = (score_scale * jnp.dot(grad_scores, key_window, preferred_element_type=jnp.float32)).astype(jnp.bfloat16)
    key_part = score_scale * lax.dot_general(grad_scores, query_flat, contract_first, preferred_element_type=jnp.float32)
    value_part = lax.dot_general(packed, grad_flat, contract_first, preferred_element_type=jnp.float32)
    attended = context.astype(jnp.bfloat16).reshape(row_count, head_count * head_width)
    return (attended, query_grad.reshape(row_count, head_count * head_width), key_part, value_part)

def reference(queries, key_vectors, value_vectors, first_values, grad_out, doc_start, mix_table, layer_index):
    row_count = TOK_DEV
    lead_rows = REACH * row_count
    key_count = lead_rows + row_count
    score_scale = 1.0 / math.sqrt(HEAD)
    attended_all = []
    query_grads = []
    key_grads = []
    value_grads = []
    first_grad = jnp.zeros((TOKENS, HEAD), jnp.float32)
    for section_index in range(N_SECTION):
        coeffs = lax.dynamic_slice_in_dim(mix_table, layer_index[section_index].astype(jnp.int32), 1, 0)[0]
        own_coef = coeffs[:HEAD]
        first_coef = coeffs[HEAD:]
        mixed_values = (own_coef * value_vectors[section_index].astype(jnp.float32) + first_coef * first_values.astype(jnp.float32)).astype(jnp.bfloat16)
        padding = jnp.zeros((lead_rows, HEAD), jnp.bfloat16)
        key_padded = jnp.concatenate([padding, key_vectors[section_index]], axis=0)
        value_padded = jnp.concatenate([padding, mixed_values], axis=0)
        section_queries = queries[section_index]
        section_grads = grad_out[section_index]

        def advance(running, block_index, section_queries=section_queries, section_grads=section_grads, key_padded=key_padded, value_padded=value_padded):
            key_sums, value_sums = running
            query_first = (block_index * row_count).astype(jnp.int32)
            attended, query_grad, key_part, value_part = window_pass(lax.dynamic_slice_in_dim(section_queries, query_first, row_count, 0), lax.dynamic_slice_in_dim(section_grads, query_first, row_count, 0), lax.dynamic_slice_in_dim(key_padded, query_first, key_count, 0), lax.dynamic_slice_in_dim(value_padded, query_first, key_count, 0), lax.dynamic_slice_in_dim(doc_start, query_first, row_count, 0), query_first, query_first - lead_rows, score_scale, HEADS)
            key_sums = lax.dynamic_update_slice_in_dim(key_sums, lax.dynamic_slice_in_dim(key_sums, query_first, key_count, 0) + key_part, query_first, 0)
            value_sums = lax.dynamic_update_slice_in_dim(value_sums, lax.dynamic_slice_in_dim(value_sums, query_first, key_count, 0) + value_part, query_first, 0)
            return ((key_sums, value_sums), (attended, query_grad))
        zero_sums = jnp.zeros((lead_rows + TOKENS, HEAD), jnp.float32)
        (key_sums, value_sums), (attended, query_grad) = lax.scan(advance, (zero_sums, zero_sums), jnp.arange(N_CTX, dtype=jnp.int32))
        mixed_grad = value_sums[lead_rows:]
        attended_all.append(attended.reshape(TOKENS, QF))
        query_grads.append(query_grad.reshape(TOKENS, QF))
        key_grads.append(key_sums[lead_rows:].astype(jnp.bfloat16))
        value_grads.append((own_coef * mixed_grad).astype(jnp.bfloat16))
        first_grad = first_grad + first_coef * mixed_grad
    return (jnp.stack(attended_all), jnp.stack(query_grads), jnp.stack(key_grads), jnp.stack(value_grads), first_grad)
```

```python
import functools
import math

import jax
import jax.numpy as jnp
from jax import lax
from jax.experimental import pallas as pl
from jax.experimental.pallas import tpu as pltpu
from jax.sharding import PartitionSpec as P

REACH = 4
BF16 = jnp.bfloat16
F32 = jnp.float32
NN = (((1,), (0,)), ((), ()))
NT = (((1,), (1,)), ((), ()))
TN = (((0,), (0,)), ((), ()))


def dot(a, b, dims=NN):
    return lax.dot_general(a, b, dims, preferred_element_type=F32)


def kernel(
    n_sec, n_ctx, rows, width, heads,
    q_hbm, k_hbm, v_hbm, f_hbm, g_hbm, start_ref, mix_ref, layer_ref,
    att_hbm, dq_hbm, kg_ref, vg_ref, fg_ref,
    q, g, att, dq, kwin, vwin, vals, firsts, packed, dscores, bias,
    vparts, kparts, vsend, ksend, vrecv, krecv, eterm, erecv,
    loc, ksem, vsem, fsem, dvsem, dksem, esem,
):
    reach = REACH
    me_s = lax.axis_index("section")
    me_c = lax.axis_index("ctx")
    scale = 1.0 / math.sqrt(width)
    own = pl.ds(reach * rows, rows)
    share = rows // n_sec

    def block(j):
        return pl.ds(j * rows, rows)

    def head(h):
        return pl.ds(h * width, width)

    def sec(r):
        return lax.rem(me_s + r, n_sec)

    def ctx(o):
        return lax.rem(me_c + o + n_ctx, n_ctx)

    in_k = pltpu.make_async_copy(k_hbm, kwin.at[own], loc.at[0])
    in_f = pltpu.make_async_copy(f_hbm, firsts.at[pl.ds(me_s * share, share)], loc.at[1])
    in_v = pltpu.make_async_copy(v_hbm, vals, loc.at[2])
    in_q = pltpu.make_async_copy(q_hbm, q, loc.at[3])
    in_g = pltpu.make_async_copy(g_hbm, g, loc.at[4])
    for c in (in_k, in_f, in_v, in_q, in_g):
        c.start()

    barrier = pltpu.get_barrier_semaphore()
    for o in range(1, reach + 1):
        for sign in (1, -1):
            pl.semaphore_signal(barrier, inc=1, device_id={"section": me_s, "ctx": ctx(sign * o)})
    for r in range(1, n_sec):
        pl.semaphore_signal(barrier, inc=1, device_id={"section": sec(r), "ctx": me_c})

    starts = start_ref[...]
    keys = (me_c - reach) * rows + lax.broadcasted_iota(jnp.int32, ((reach + 1) * rows, rows), 0)
    queries = me_c * rows + lax.broadcasted_iota(jnp.int32, ((reach + 1) * rows, rows), 1)
    turned = jnp.where((keys >= starts) & (keys <= queries), 0.0, -jnp.inf).astype(F32)
    for j in range(reach + 1):
        bias[:, block(j)] = turned[j * rows : (j + 1) * rows].T

    coeffs = mix_ref[pl.ds(layer_ref[0], 1), :]
    own_coef = coeffs[:, :width]
    first_coef = coeffs[:, width:]

    in_k.wait()
    in_f.wait()
    pl.semaphore_wait(barrier, 2 * reach + n_sec - 1)

    k_out = [
        pltpu.make_async_remote_copy(
            kwin.at[own], kwin.at[block(reach - o)], ksem.at[0, o], ksem.at[1, o],
            device_id={"section": me_s, "ctx": ctx(o)})
        for o in range(1, reach + 1)
    ]
    f_out = [
        pltpu.make_async_remote_copy(
            firsts.at[pl.ds(me_s * share, share)], firsts.at[pl.ds(me_s * share, share)],
            fsem.at[0, r], fsem.at[1, r],
            device_id={"section": sec(r), "ctx": me_c})
        for r in range(1, n_sec)
    ]
    v_out = [
        pltpu.make_async_remote_copy(
            vwin.at[own], vwin.at[block(reach - o)], vsem.at[0, o], vsem.at[1, o],
            device_id={"section": me_s, "ctx": ctx(o)})
        for o in range(1, reach + 1)
    ]
    dv_out = [
        pltpu.make_async_remote_copy(
            vsend.at[block(reach - o)], vrecv.at[o - 1], dvsem.at[0, o], dvsem.at[1, o],
            device_id={"section": me_s, "ctx": ctx(-o)})
        for o in range(1, reach + 1)
    ]
    dk_out = [
        pltpu.make_async_remote_copy(
            ksend.at[block(reach - o)], krecv.at[o - 1], dksem.at[0, o], dksem.at[1, o],
            device_id={"section": me_s, "ctx": ctx(-o)})
        for o in range(1, reach + 1)
    ]
    e_out = [
        pltpu.make_async_remote_copy(
            eterm.at[pl.ds(sec(r) * share, share)], erecv.at[r], esem.at[0, r], esem.at[1, r],
            device_id={"section": sec(r), "ctx": me_c})
        for r in range(1, n_sec)
    ]
    for c in f_out:
        c.start()
    for c in k_out:
        c.start()

    in_v.wait()
    for c in f_out:
        c.wait_recv()
    vwin[own, :] = (own_coef * vals[...].astype(F32) + first_coef * firsts[...].astype(F32)).astype(BF16)
    for c in v_out:
        c.start()

    in_q.wait()
    for c in k_out:
        c.wait_recv()
    for h in range(heads):
        s = dot(q[:, head(h)], kwin[...], NT) + bias[...]
        top = jnp.max(s, axis=1, keepdims=True)
        e = jnp.exp((s - top) * scale)
        total = jnp.sum(e, axis=1, keepdims=True)
        packed[h] = (e * (1.0 / total)).astype(BF16)

    in_g.wait()
    vparts[...] = dot(
        jnp.concatenate([g[:, head(h)] for h in range(heads)], axis=0),
        packed[...].reshape(heads * rows, (reach + 1) * rows), TN)
    for j in range(reach):
        vsend[block(j), :] = vparts[:, block(j)].T.astype(BF16)
    for c in reversed(dv_out):
        c.start()

    for c in v_out:
        c.wait_recv()
    for h in range(heads):
        p = packed[h]
        c = dot(p, vwin[...])
        att[:, head(h)] = c.astype(BF16)
        gh = g[:, head(h)]
        row_dot = jnp.sum(gh.astype(F32) * c, axis=1, keepdims=True)
        dp = dot(gh, vwin[...], NT)
        dscores[h] = (p.astype(F32) * (dp - row_dot)).astype(BF16)
    out_att = pltpu.make_async_copy(att, att_hbm, loc.at[5])
    out_att.start()

    kparts[...] = scale * dot(
        jnp.concatenate([q[:, head(h)] for h in range(heads)], axis=0),
        dscores[...].reshape(heads * rows, (reach + 1) * rows), TN)
    for j in range(reach):
        ksend[block(j), :] = kparts[:, block(j)].T.astype(BF16)
    for c in reversed(dk_out):
        c.start()

    mixed_grad = vparts[:, own].T
    for c in dv_out:
        c.wait_recv()
    for o in range(reach):
        mixed_grad = mixed_grad + vrecv[o].astype(F32)
    vg_ref[...] = (own_coef * mixed_grad).astype(BF16)
    eterm[...] = first_coef * mixed_grad
    for c in e_out:
        c.start()

    for h in range(heads):
        dq[:, head(h)] = (scale * dot(dscores[h], kwin[...])).astype(BF16)
    out_dq = pltpu.make_async_copy(dq, dq_hbm, loc.at[6])
    out_dq.start()

    key_grad = kparts[:, own].T
    for c in dk_out:
        c.wait_recv()
    for o in range(reach):
        key_grad = key_grad + krecv[o].astype(F32)
    kg_ref[...] = key_grad.astype(BF16)

    for c in e_out:
        c.wait_recv()
    first_grad = eterm[pl.ds(me_s * share, share), :]
    for r in range(1, n_sec):
        first_grad = first_grad + erecv[r]
    fg_ref[...] = first_grad

    for c in k_out + f_out + v_out + dv_out + dk_out + e_out:
        c.wait_send()
    out_att.wait()
    out_dq.wait()


def solution(mesh):
    n_sec, n_ctx = mesh.shape["section"], mesh.shape["ctx"]

    def per_device(queries, keys, values, firsts, grads, starts, mix_table, layer_index):
        rows, width = keys.shape[1], keys.shape[2]
        feats = queries.shape[2]
        heads = feats // width
        share = firsts.shape[0]
        window = (REACH + 1) * rows
        hbm = pl.BlockSpec(memory_space=pl.ANY)
        vmem = pl.BlockSpec(memory_space=pltpu.VMEM)
        smem = pl.BlockSpec(memory_space=pltpu.SMEM)
        att, dq, kg, vg, fg = pl.pallas_call(
            functools.partial(kernel, n_sec, n_ctx, rows, width, heads),
            out_shape=[
                jax.ShapeDtypeStruct((rows, feats), BF16),
                jax.ShapeDtypeStruct((rows, feats), BF16),
                jax.ShapeDtypeStruct((rows, width), BF16),
                jax.ShapeDtypeStruct((rows, width), BF16),
                jax.ShapeDtypeStruct((share, width), F32),
            ],
            in_specs=[hbm, hbm, hbm, hbm, hbm, vmem, vmem, smem],
            out_specs=[hbm, hbm, vmem, vmem, vmem],
            scratch_shapes=[
                pltpu.VMEM((rows, feats), BF16),
                pltpu.VMEM((rows, feats), BF16),
                pltpu.VMEM((rows, feats), BF16),
                pltpu.VMEM((rows, feats), BF16),
                pltpu.VMEM((window, width), BF16),
                pltpu.VMEM((window, width), BF16),
                pltpu.VMEM((rows, width), BF16),
                pltpu.VMEM((rows, width), BF16),
                pltpu.VMEM((heads, rows, window), BF16),
                pltpu.VMEM((heads, rows, window), BF16),
                pltpu.VMEM((rows, window), F32),
                pltpu.VMEM((width, window), F32),
                pltpu.VMEM((width, window), F32),
                pltpu.VMEM((REACH * rows, width), BF16),
                pltpu.VMEM((REACH * rows, width), BF16),
                pltpu.VMEM((REACH, rows, width), BF16),
                pltpu.VMEM((REACH, rows, width), BF16),
                pltpu.VMEM((rows, width), F32),
                pltpu.VMEM((n_sec, share, width), F32),
                pltpu.SemaphoreType.DMA((7,)),
                pltpu.SemaphoreType.DMA((2, REACH + 1)),
                pltpu.SemaphoreType.DMA((2, REACH + 1)),
                pltpu.SemaphoreType.DMA((2, n_sec)),
                pltpu.SemaphoreType.DMA((2, REACH + 1)),
                pltpu.SemaphoreType.DMA((2, REACH + 1)),
                pltpu.SemaphoreType.DMA((2, n_sec)),
            ],
            compiler_params=pltpu.CompilerParams(
                collective_id=0, has_side_effects=True, vmem_limit_bytes=48 << 20),
            cost_estimate=pl.CostEstimate(
                flops=12 * rows * feats * window, bytes_accessed=8 * rows * feats,
                transcendentals=rows * heads * window),
            name="attention",
        )(queries[0], keys[0], values[0], firsts, grads[0], starts.reshape(1, rows), mix_table, layer_index)
        return att[None], dq[None], kg[None], vg[None], fg

    return jax.shard_map(
        per_device,
        mesh=mesh,
        in_specs=(
            P("section", "ctx", None),
            P("section", "ctx", None),
            P("section", "ctx", None),
            P(("ctx", "section"), None),
            P("section", "ctx", None),
            P("ctx"),
            P(),
            P("section"),
        ),
        out_specs=(
            P("section", "ctx", None),
            P("section", "ctx", None),
            P("section", "ctx", None),
            P("section", "ctx", None),
            P(("ctx", "section"), None),
        ),
        check_vma=False,
    )
```

```python
import functools
import math

import jax
import jax.numpy as jnp
from jax import lax
from jax.experimental import pallas as pl
from jax.experimental.pallas import tpu as pltpu
from jax.sharding import PartitionSpec as P

REACH = 4
BF16 = jnp.bfloat16
F32 = jnp.float32
NN = (((1,), (0,)), ((), ()))
NT = (((1,), (1,)), ((), ()))
TN = (((0,), (0,)), ((), ()))


def dot(a, b, dims=NN):
    return lax.dot_general(a, b, dims, preferred_element_type=F32)


def kernel(
    n_sec, n_ctx, rows, width, heads,
    q_hbm, k_hbm, v_hbm, f_hbm, g_hbm, start_hbm, mix_hbm, layer_ref,
    att, dq, kg, vg, fg,
    q, g, kwin, vwin, vraw, fpart, fall, starts, mix, packed, dscores, bias,
    vparts, kparts, vhome, khome, vpair, kpair, vback, kback, rsend, rrecv, rhome, rback,
    loc, ksem, vsem, fzsem, fssem, dvsem, dksem, essem, rzsem,
):
    me_s = lax.axis_index("section")
    me_c = lax.axis_index("ctx")
    odd = lax.rem(me_c, 2)
    scale = 1.0 / math.sqrt(width)
    share = rows // n_sec
    mine = (0, 2, 4)

    def block(j):
        return pl.ds(j * rows, rows)

    def part(b):
        return pl.ds(b * share, share)

    def head(h):
        return pl.ds(h * width, width)

    def at_sec(r):
        return {"section": lax.rem(me_s + r, n_sec), "ctx": me_c}

    def at_ctx(o):
        return {"section": me_s, "ctx": me_c + o}

    mate = {"section": me_s, "ctx": me_c + 1 - 2 * odd}
    own = block(REACH)
    near = pl.ds((4 - 2 * odd) * rows, rows)
    far = pl.ds((2 - 2 * odd) * rows, rows)

    def remote(src, dst, sems, i, device):
        return pltpu.make_async_remote_copy(src, dst, sems.at[0, i], sems.at[1, i], device_id=device)

    loads = [
        pltpu.make_async_copy(a, b, loc.at[i])
        for i, (a, b) in enumerate([
            (k_hbm, kwin.at[own]),
            (f_hbm, fpart.at[part(2)]),
            (v_hbm, vraw.at[own]),
            (start_hbm, starts),
            (mix_hbm, mix),
            (q_hbm, q),
            (g_hbm, g),
        ])
    ]
    in_k, in_f, in_v, in_start, in_mix, in_q, in_g = loads

    back2, back4 = me_c >= 2, me_c >= 4
    on2, on4 = me_c + 2 < n_ctx, me_c + 4 < n_ctx

    barrier = pltpu.get_barrier_semaphore()
    for there, o in ((on4, 4), (on2, 2), (back2, -2), (back4, -4)):
        @pl.when(there)
        def _():
            pl.semaphore_signal(barrier, inc=1, device_id=at_ctx(o))
    pl.semaphore_signal(barrier, inc=1, device_id=mate)
    for r in range(1, n_sec):
        pl.semaphore_signal(barrier, inc=1, device_id=at_sec(r))
    for c in loads:
        c.start()

    fz1 = remote(f_hbm, fpart.at[part(1)], fzsem, 0, at_ctx(2))
    fz2 = remote(f_hbm, fpart.at[part(0)], fzsem, 1, at_ctx(4))
    fs = [remote(fpart, fall.at[me_s], fssem, r, at_sec(r)) for r in range(1, n_sec)]
    k1 = remote(k_hbm, kwin.at[block(2)], ksem, 0, at_ctx(2))
    k2 = remote(k_hbm, kwin.at[block(0)], ksem, 1, at_ctx(4))
    k3 = remote(kwin.at[near], kwin.at[block(3)], ksem, 2, mate)
    k4 = remote(kwin.at[far], kwin.at[block(1)], ksem, 3, mate)
    v1 = remote(v_hbm, vraw.at[block(2)], vsem, 0, at_ctx(2))
    v2 = remote(v_hbm, vraw.at[block(0)], vsem, 1, at_ctx(4))
    v3 = remote(vwin.at[near], vwin.at[block(3)], vsem, 2, mate)
    v4 = remote(vwin.at[far], vwin.at[block(1)], vsem, 3, mate)
    dv1 = remote(vhome.at[block(2)], vback.at[0], dvsem, 0, at_ctx(-2))
    dv2 = remote(vhome.at[block(0)], vback.at[1], dvsem, 1, at_ctx(-4))
    dv3 = remote(vhome.at[block(3)], vpair.at[0], dvsem, 2, mate)
    dv4 = remote(vhome.at[block(1)], vpair.at[1], dvsem, 3, mate)
    dk1 = remote(khome.at[block(2)], kback.at[0], dksem, 0, at_ctx(-2))
    dk2 = remote(khome.at[block(0)], kback.at[1], dksem, 1, at_ctx(-4))
    dk3 = remote(khome.at[block(3)], kpair.at[0], dksem, 2, mate)
    dk4 = remote(khome.at[block(1)], kpair.at[1], dksem, 3, mate)
    es = [remote(rsend.at[lax.rem(me_s + r, n_sec)], rrecv.at[r], essem, r, at_sec(r)) for r in range(1, n_sec)]
    rz1 = remote(rhome.at[part(1)], rback.at[0], rzsem, 0, at_ctx(-2))
    rz2 = remote(rhome.at[part(0)], rback.at[1], rzsem, 1, at_ctx(-4))

    @pl.when(jnp.logical_not(back4))
    def _():
        for ref, size in ((kwin, rows), (vraw, rows), (fpart, share)):
            ref[pl.ds(0, size), :] = jnp.zeros((size, width), BF16)

    @pl.when(jnp.logical_not(back2))
    def _():
        for ref, lo, size in ((kwin, 2 * rows, rows), (vraw, 2 * rows, rows), (fpart, share, share)):
            ref[pl.ds(lo, size), :] = jnp.zeros((size, width), BF16)

    for there, i in ((on2, 0), (on4, 1)):
        @pl.when(jnp.logical_not(there))
        def _():
            for ref in (vback, kback, rback):
                ref[i] = jnp.zeros(ref.shape[1:], ref.dtype)

    def near_far(there2, there4, *actions):
        for act2, act4 in actions:
            pl.when(there4)(act4)
            pl.when(there2)(act2)

    ahead = lax.convert_element_type(on2, jnp.int32) + lax.convert_element_type(on4, jnp.int32)
    behind = lax.convert_element_type(back2, jnp.int32) + lax.convert_element_type(back4, jnp.int32)
    pl.semaphore_wait(barrier, n_sec + ahead + behind)
    near_far(on2, on4, (fz1.start, fz2.start), (k1.start, k2.start), (v1.start, v2.start))
    in_k.wait()

    @pl.when(odd == 0)
    def _():
        k3.start()

    in_start.wait()
    window = (REACH + 1) * rows
    key_at = (me_c - REACH) * rows + lax.broadcasted_iota(jnp.int32, (window, rows), 0)
    query_at = me_c * rows + lax.broadcasted_iota(jnp.int32, (window, rows), 1)
    turned = jnp.where((key_at >= starts[...]) & (key_at <= query_at), 0.0, -jnp.inf).astype(F32)
    for j in range(REACH + 1):
        bias[:, block(j)] = turned[j * rows : (j + 1) * rows].T

    in_mix.wait()
    coeffs = mix[pl.ds(layer_ref[0], 1), :]
    own_coef = coeffs[:, :width]
    first_coef = coeffs[:, width:]

    in_f.wait()

    @pl.when(back2)
    def _():
        k1.wait_recv()

    @pl.when(odd == 0)
    def _():
        k4.start()

    @pl.when(odd == 1)
    def _():
        k3.start()

    near_far(back2, back4, (fz1.wait_recv, fz2.wait_recv))
    for c in fs:
        c.start()
    in_q.wait()

    @pl.when(back4)
    def _():
        k2.wait_recv()

    @pl.when(odd == 1)
    def _():
        k4.start()

    k3.wait_recv()
    k4.wait_recv()
    for h in range(heads):
        s = dot(q[:, head(h)], kwin[...], NT) + bias[...]
        top = jnp.max(s, axis=1, keepdims=True)
        e = jnp.exp((s - top) * scale)
        total = jnp.sum(e, axis=1, keepdims=True)
        packed[h] = (e * (1.0 / total)).astype(BF16)

    in_v.wait()
    near_far(back2, back4, (v1.wait_recv, v2.wait_recv))
    fall[me_s] = fpart[...]
    for c in fs:
        c.wait_recv()
    for b in (2, 1, 0):
        firsts = jnp.concatenate([fall[s, b * share : (b + 1) * share, :] for s in range(n_sec)], axis=0)
        vwin[block(mine[b]), :] = (
            own_coef * vraw[block(mine[b]), :].astype(F32) + first_coef * firsts.astype(F32)
        ).astype(BF16)
    v3.start()
    v4.start()

    in_g.wait()
    g_rows = jnp.concatenate([g[:, head(h)] for h in range(heads)], axis=0)
    for lo, hi in ((0, 2), (2, 4), (4, 5)):
        turned_sum = dot(g_rows, packed[:, :, lo * rows : hi * rows].reshape(heads * rows, (hi - lo) * rows), TN)
        for j in range(lo, hi):
            vparts[block(j), :] = turned_sum[:, (j - lo) * rows : (j - lo + 1) * rows].T
        if lo == 0:
            vhome[block(1), :] = vparts[block(1), :].astype(BF16)
            dv4.start()
        if lo == 2:
            vhome[block(3), :] = vparts[block(3), :].astype(BF16)
            dv3.start()
    v3.wait_recv()
    v4.wait_recv()

    for h in range(heads):
        if h == heads // 2:
            dv4.wait_recv()
            dv3.wait_recv()
            vparts[far, :] = vparts[far, :] + vpair[1].astype(F32)
            vparts[near, :] = vparts[near, :] + vpair[0].astype(F32)
            vhome[block(0), :] = vparts[block(0), :].astype(BF16)
            vhome[block(2), :] = vparts[block(2), :].astype(BF16)
            near_far(back2, back4, (dv1.start, dv2.start))
            for b in range(3):
                term = (first_coef * vparts[block(mine[b]), :]).astype(BF16)
                for s in range(n_sec):
                    rsend[s, b * share : (b + 1) * share, :] = term[s * share : (s + 1) * share]
            for c in es:
                c.start()
        p = packed[h]
        c = dot(p, vwin[...])
        att[:, head(h)] = c.astype(BF16)
        gh = g[:, head(h)]
        row_dot = jnp.sum(gh.astype(F32) * c, axis=1, keepdims=True)
        dp = dot(gh, vwin[...], NT)
        dscores[h] = (p.astype(F32) * (dp - row_dot)).astype(BF16)

    q_rows = jnp.concatenate([q[:, head(h)] for h in range(heads)], axis=0)
    for lo, hi in ((0, 2), (2, 4), (4, 5)):
        turned_sum = scale * dot(
            q_rows, dscores[:, :, lo * rows : hi * rows].reshape(heads * rows, (hi - lo) * rows), TN)
        for j in range(lo, hi):
            kparts[block(j), :] = turned_sum[:, (j - lo) * rows : (j - lo + 1) * rows].T
        if lo == 0:
            khome[block(1), :] = kparts[block(1), :].astype(BF16)
            dk4.start()
        if lo == 2:
            khome[block(3), :] = kparts[block(3), :].astype(BF16)
            dk3.start()
    dk4.wait_recv()
    dk3.wait_recv()
    kparts[far, :] = kparts[far, :] + kpair[1].astype(F32)
    kparts[near, :] = kparts[near, :] + kpair[0].astype(F32)
    khome[block(0), :] = kparts[block(0), :].astype(BF16)
    khome[block(2), :] = kparts[block(2), :].astype(BF16)
    near_far(back2, back4, (dk1.start, dk2.start))

    for c in es:
        c.wait_recv()
    total = rsend[me_s].astype(F32)
    for r in range(1, n_sec):
        total = total + rrecv[r].astype(F32)
    rhome[...] = total
    near_far(back2, back4, (rz1.start, rz2.start))

    near_far(on2, on4, (dv1.wait_recv, dv2.wait_recv))
    vg[...] = (own_coef * (vparts[own, :] + vback[0].astype(F32) + vback[1].astype(F32))).astype(BF16)

    for h in range(heads):
        dq[:, head(h)] = (scale * dot(dscores[h], kwin[...])).astype(BF16)

    near_far(on2, on4, (rz1.wait_recv, rz2.wait_recv))
    fg[...] = rhome[part(2), :] + rback[0] + rback[1]
    near_far(on2, on4, (dk1.wait_recv, dk2.wait_recv))
    kg[...] = (kparts[own, :] + kback[0].astype(F32) + kback[1].astype(F32)).astype(BF16)

    for c in fs + es + [k3, k4, v3, v4, dv3, dv4, dk3, dk4]:
        c.wait_send()
    near_far(on2, on4, *[(a.wait_send, b.wait_send) for a, b in ((fz1, fz2), (k1, k2), (v1, v2))])
    near_far(back2, back4, *[(a.wait_send, b.wait_send) for a, b in ((dv1, dv2), (dk1, dk2), (rz1, rz2))])


def place(*refs):
    n = (len(refs) - 1) // 2
    copies = [pltpu.make_async_copy(refs[i], refs[n + i], refs[-1].at[i]) for i in range(n)]
    for c in copies:
        c.start()
    for c in copies:
        c.wait()


def solution(mesh):
    n_sec, n_ctx = mesh.shape["section"], mesh.shape["ctx"]

    def per_device(queries, keys, values, firsts, grads, starts, mix_table, layer_index):
        rows, width = keys.shape[1], keys.shape[2]
        feats = queries.shape[2]
        heads = feats // width
        share = firsts.shape[0]
        window = (REACH + 1) * rows
        piece = 3 * share
        hbm = pl.BlockSpec(memory_space=pltpu.HBM)
        anyw = pl.BlockSpec(memory_space=pl.ANY)
        smem = pl.BlockSpec(memory_space=pltpu.SMEM)
        vmem = pl.BlockSpec(memory_space=pltpu.VMEM)
        shapes = [
            jax.ShapeDtypeStruct((rows, feats), BF16),
            jax.ShapeDtypeStruct((rows, feats), BF16),
            jax.ShapeDtypeStruct((rows, width), BF16),
            jax.ShapeDtypeStruct((rows, width), BF16),
            jax.ShapeDtypeStruct((share, width), F32),
        ]
        four = pltpu.SemaphoreType.DMA((2, 4))
        two = pltpu.SemaphoreType.DMA((2, 2))
        results = pl.pallas_call(
            functools.partial(kernel, n_sec, n_ctx, rows, width, heads),
            out_shape=[pltpu.VMEM(x.shape, x.dtype) for x in shapes],
            in_specs=[hbm] * 7 + [smem],
            out_specs=[vmem] * 5,
            scratch_shapes=[
                pltpu.VMEM((rows, feats), BF16),
                pltpu.VMEM((rows, feats), BF16),
                pltpu.VMEM((window, width), BF16),
                pltpu.VMEM((window, width), BF16),
                pltpu.VMEM((window, width), BF16),
                pltpu.VMEM((piece, width), BF16),
                pltpu.VMEM((n_sec, piece, width), BF16),
                pltpu.VMEM((1, rows), jnp.int32),
                pltpu.VMEM(mix_table.shape, F32),
                pltpu.VMEM((heads, rows, window), BF16),
                pltpu.VMEM((heads, rows, window), BF16),
                pltpu.VMEM((rows, window), F32),
                pltpu.VMEM((window, width), F32),
                pltpu.VMEM((window, width), F32),
                pltpu.VMEM((REACH * rows, width), BF16),
                pltpu.VMEM((REACH * rows, width), BF16),
                pltpu.VMEM((2, rows, width), BF16),
                pltpu.VMEM((2, rows, width), BF16),
                pltpu.VMEM((2, rows, width), BF16),
                pltpu.VMEM((2, rows, width), BF16),
                pltpu.VMEM((n_sec, piece, width), BF16),
                pltpu.VMEM((n_sec, piece, width), BF16),
                pltpu.VMEM((piece, width), F32),
                pltpu.VMEM((2, share, width), F32),
                pltpu.SemaphoreType.DMA((7,)),
                four,
                four,
                two,
                pltpu.SemaphoreType.DMA((2, n_sec)),
                four,
                four,
                pltpu.SemaphoreType.DMA((2, n_sec)),
                two,
            ],
            compiler_params=pltpu.CompilerParams(
                collective_id=0, has_side_effects=True, vmem_limit_bytes=48 << 20),
            cost_estimate=pl.CostEstimate(
                flops=12 * rows * feats * window, bytes_accessed=8 * rows * feats,
                transcendentals=rows * heads * window),
            name="attention",
        )(*[
            pltpu.with_memory_space_constraint(x, pltpu.HBM)
            for x in (queries[0], keys[0], values[0], firsts, grads[0], starts.reshape(1, rows), mix_table)
        ], layer_index)
        att, dq, kg, vg, fg = pl.pallas_call(
            place,
            out_shape=shapes,
            in_specs=[anyw] * 5,
            out_specs=[hbm] * 5,
            scratch_shapes=[pltpu.SemaphoreType.DMA((5,))],
            compiler_params=pltpu.CompilerParams(vmem_limit_bytes=8 << 20),
            name="place",
        )(*results)
        return att[None], dq[None], kg[None], vg[None], fg

    return jax.shard_map(
        per_device,
        mesh=mesh,
        in_specs=(
            P("section", "ctx", None),
            P("section", "ctx", None),
            P("section", "ctx", None),
            P(("ctx", "section"), None),
            P("section", "ctx", None),
            P("ctx"),
            P(),
            P("section"),
        ),
        out_specs=(
            P("section", "ctx", None),
            P("section", "ctx", None),
            P("section", "ctx", None),
            P("section", "ctx", None),
            P(("ctx", "section"), None),
        ),
        check_vma=False,
    )
```

```python
import functools
import math

import jax
import jax.numpy as jnp
from jax import lax
from jax.experimental import pallas as pl
from jax.experimental.pallas import tpu as pltpu
from jax.sharding import PartitionSpec as P

REACH = 4
BF16 = jnp.bfloat16
F32 = jnp.float32
NN = (((1,), (0,)), ((), ()))
NT = (((1,), (1,)), ((), ()))


def dot(a, b, dims=NN):
    return lax.dot_general(a, b, dims, preferred_element_type=F32)


def kernel(
    n_sec, n_ctx, rows, width, heads,
    q_hbm, k_hbm, v_hbm, f_hbm, g_hbm, start_hbm, mix_hbm, layer_ref,
    att, dq, kg, vg, fg,
    q, g, kwin, vwin, vraw, fpart, fall, starts, mix, packed, dscores, bias,
    q_turned, g_turned, early, early_top, early_sum,
    vparts, kparts, vhome, khome, vpair, kpair, vback, kback, rsend, rrecv, rhome, rback,
    loc, ksem, vsem, fzsem, fssem, dvsem, dksem, essem, rzsem,
):
    me_s = lax.axis_index("section")
    me_c = lax.axis_index("ctx")
    odd = lax.rem(me_c, 2)
    scale = 1.0 / math.sqrt(width)
    share = rows // n_sec
    mine = (0, 2, 4)

    def block(j):
        return pl.ds(j * rows, rows)

    def part(b):
        return pl.ds(b * share, share)

    def head(h):
        return pl.ds(h * width, width)

    def at_sec(r):
        return {"section": lax.rem(me_s + r, n_sec), "ctx": me_c}

    def at_ctx(o):
        return {"section": me_s, "ctx": me_c + o}

    mate = {"section": me_s, "ctx": me_c + 1 - 2 * odd}
    own = block(REACH)
    near = pl.ds((4 - 2 * odd) * rows, rows)
    far = pl.ds((2 - 2 * odd) * rows, rows)

    def remote(src, dst, sems, i, device):
        return pltpu.make_async_remote_copy(src, dst, sems.at[0, i], sems.at[1, i], device_id=device)

    loads = [
        pltpu.make_async_copy(a, b, loc.at[i])
        for i, (a, b) in enumerate([
            (k_hbm, kwin.at[own]),
            (f_hbm, fpart.at[part(2)]),
            (v_hbm, vraw.at[own]),
            (start_hbm, starts),
            (mix_hbm, mix),
            (q_hbm, q),
            (g_hbm, g),
        ])
    ]
    in_k, in_f, in_v, in_start, in_mix, in_q, in_g = loads

    back2, back4 = me_c >= 2, me_c >= 4
    on2, on4 = me_c + 2 < n_ctx, me_c + 4 < n_ctx

    barrier = pltpu.get_barrier_semaphore()
    for there, o in ((on4, 4), (on2, 2), (back2, -2), (back4, -4)):
        @pl.when(there)
        def _():
            pl.semaphore_signal(barrier, inc=1, device_id=at_ctx(o))
    pl.semaphore_signal(barrier, inc=1, device_id=mate)
    for r in range(1, n_sec):
        pl.semaphore_signal(barrier, inc=1, device_id=at_sec(r))
    for c in loads:
        c.start()

    fz1 = remote(f_hbm, fpart.at[part(1)], fzsem, 0, at_ctx(2))
    fz2 = remote(f_hbm, fpart.at[part(0)], fzsem, 1, at_ctx(4))
    fs = [remote(fpart, fall.at[me_s], fssem, r, at_sec(r)) for r in range(1, n_sec)]
    k1 = remote(k_hbm, kwin.at[block(2)], ksem, 0, at_ctx(2))
    k2 = remote(k_hbm, kwin.at[block(0)], ksem, 1, at_ctx(4))
    k3 = remote(kwin.at[near], kwin.at[block(3)], ksem, 2, mate)
    k4 = remote(kwin.at[far], kwin.at[block(1)], ksem, 3, mate)
    v1 = remote(v_hbm, vraw.at[block(2)], vsem, 0, at_ctx(2))
    v2 = remote(v_hbm, vraw.at[block(0)], vsem, 1, at_ctx(4))
    v3 = remote(vwin.at[near], vwin.at[block(3)], vsem, 2, mate)
    v4 = remote(vwin.at[far], vwin.at[block(1)], vsem, 3, mate)
    dv1 = remote(vhome.at[block(2)], vback.at[0], dvsem, 0, at_ctx(-2))
    dv2 = remote(vhome.at[block(0)], vback.at[1], dvsem, 1, at_ctx(-4))
    dv3 = remote(vhome.at[block(3)], vpair.at[0], dvsem, 2, mate)
    dv4 = remote(vhome.at[block(1)], vpair.at[1], dvsem, 3, mate)
    dk1 = remote(khome.at[block(2)], kback.at[0], dksem, 0, at_ctx(-2))
    dk2 = remote(khome.at[block(0)], kback.at[1], dksem, 1, at_ctx(-4))
    dk3 = remote(khome.at[block(3)], kpair.at[0], dksem, 2, mate)
    dk4 = remote(khome.at[block(1)], kpair.at[1], dksem, 3, mate)
    es = [remote(rsend.at[lax.rem(me_s + r, n_sec)], rrecv.at[r], essem, r, at_sec(r)) for r in range(1, n_sec)]
    rz1 = remote(rhome.at[part(1)], rback.at[0], rzsem, 0, at_ctx(-2))
    rz2 = remote(rhome.at[part(0)], rback.at[1], rzsem, 1, at_ctx(-4))

    @pl.when(jnp.logical_not(back4))
    def _():
        for ref, size in ((kwin, rows), (vraw, rows), (fpart, share)):
            ref[pl.ds(0, size), :] = jnp.zeros((size, width), BF16)

    @pl.when(jnp.logical_not(back2))
    def _():
        for ref, lo, size in ((kwin, 2 * rows, rows), (vraw, 2 * rows, rows), (fpart, share, share)):
            ref[pl.ds(lo, size), :] = jnp.zeros((size, width), BF16)

    for there, i in ((on2, 0), (on4, 1)):
        @pl.when(jnp.logical_not(there))
        def _():
            for ref in (vback, kback, rback):
                ref[i] = jnp.zeros(ref.shape[1:], ref.dtype)

    def near_far(there2, there4, *actions):
        for act2, act4 in actions:
            pl.when(there4)(act4)
            pl.when(there2)(act2)

    in_q.wait()
    for h in range(heads):
        q_turned[:, head(h)] = q[:, head(h)].T
    in_g.wait()
    for h in range(heads):
        g_turned[:, head(h)] = g[:, head(h)].T
    ahead = lax.convert_element_type(on2, jnp.int32) + lax.convert_element_type(on4, jnp.int32)
    behind = lax.convert_element_type(back2, jnp.int32) + lax.convert_element_type(back4, jnp.int32)
    pl.semaphore_wait(barrier, n_sec + ahead + behind)
    near_far(on2, on4, (fz1.start, fz2.start), (k1.start, k2.start))
    in_k.wait()

    @pl.when(odd == 0)
    def _():
        k3.start()

    in_start.wait()
    window = (REACH + 1) * rows
    key_at = (me_c - REACH) * rows + lax.broadcasted_iota(jnp.int32, (window, rows), 0)
    query_at = me_c * rows + lax.broadcasted_iota(jnp.int32, (window, rows), 1)
    turned = jnp.where((key_at >= starts[...]) & (key_at <= query_at), 0.0, -jnp.inf).astype(F32)
    for j in range(REACH + 1):
        bias[:, block(j)] = turned[j * rows : (j + 1) * rows].T

    in_mix.wait()
    coeffs = mix[pl.ds(layer_ref[0], 1), :]
    own_coef = coeffs[:, :width]
    first_coef = coeffs[:, width:]

    in_f.wait()

    @pl.when(back2)
    def _():
        k1.wait_recv()

    @pl.when(odd == 0)
    def _():
        k4.start()

    @pl.when(odd == 1)
    def _():
        k3.start()

    near_far(on2, on4, (v1.start, v2.start))
    near_far(back2, back4, (fz1.wait_recv, fz2.wait_recv))
    for c in fs:
        c.start()
    for h in range(heads):
        qh = q[:, head(h)]
        s4 = dot(qh, kwin[block(4), :], NT) + bias[:, block(4)]
        s2 = dot(qh, kwin[block(2), :], NT) + bias[:, block(2)]
        top = jnp.max(jnp.maximum(s4, s2), axis=1, keepdims=True)
        e4 = jnp.exp((s4 - top) * scale)
        e2 = jnp.exp((s2 - top) * scale)
        early[h, :, :rows] = e2
        early[h, :, rows:] = e4
        early_top[h] = jnp.broadcast_to(top, (rows, width))
        early_sum[h] = jnp.broadcast_to(jnp.sum(e4 + e2, axis=1, keepdims=True), (rows, width))

    @pl.when(back4)
    def _():
        k2.wait_recv()

    @pl.when(odd == 1)
    def _():
        k4.start()

    k3.wait_recv()
    k4.wait_recv()
    for h in range(heads):
        qh = q[:, head(h)]
        s0 = dot(qh, kwin[pl.ds(0, 2 * rows), :], NT) + bias[:, : 2 * rows]
        s3 = dot(qh, kwin[block(3), :], NT) + bias[:, block(3)]
        late_top = jnp.max(jnp.maximum(jnp.maximum(s0[:, :rows], s0[:, rows:]), s3), axis=1, keepdims=True)
        top = jnp.maximum(early_top[h], late_top)
        e0 = jnp.exp((s0[:, :rows] - top) * scale)
        e1 = jnp.exp((s0[:, rows:] - top) * scale)
        e3 = jnp.exp((s3 - top) * scale)
        fade = jnp.exp((early_top[h] - top) * scale)
        inverse = 1.0 / (jnp.sum(e0 + e1 + e3, axis=1, keepdims=True) + early_sum[h] * fade)
        fade = fade * inverse
        packed[h, :, block(0)] = (e0 * inverse).astype(BF16)
        packed[h, :, block(1)] = (e1 * inverse).astype(BF16)
        packed[h, :, block(2)] = (early[h, :, :rows] * fade).astype(BF16)
        packed[h, :, block(3)] = (e3 * inverse).astype(BF16)
        packed[h, :, block(4)] = (early[h, :, rows:] * fade).astype(BF16)

    in_v.wait()
    near_far(back2, back4, (v1.wait_recv, v2.wait_recv))
    fall[me_s] = fpart[...]
    for c in fs:
        c.wait_recv()
    for b in (2, 1, 0):
        firsts = jnp.concatenate([fall[s, b * share : (b + 1) * share, :] for s in range(n_sec)], axis=0)
        vwin[block(mine[b]), :] = (
            own_coef * vraw[block(mine[b]), :].astype(F32) + first_coef * firsts.astype(F32)
        ).astype(BF16)
    v3.start()
    v4.start()

    for lo, hi in ((0, 2), (2, 4), (4, 5)):
        turned_sum = dot(g_turned[...], packed[:, :, lo * rows : hi * rows].reshape(heads * rows, (hi - lo) * rows))
        for j in range(lo, hi):
            vparts[block(j), :] = turned_sum[:, (j - lo) * rows : (j - lo + 1) * rows].T
        if lo == 0:
            vhome[block(1), :] = vparts[block(1), :].astype(BF16)
            dv4.start()
        if lo == 2:
            vhome[block(3), :] = vparts[block(3), :].astype(BF16)
            dv3.start()
    v3.wait_recv()
    v4.wait_recv()

    for h in range(heads):
        if h == heads // 4:
            dv4.wait_recv()
            dv3.wait_recv()
            vparts[far, :] = vparts[far, :] + vpair[1].astype(F32)
            vparts[near, :] = vparts[near, :] + vpair[0].astype(F32)
            vhome[block(0), :] = vparts[block(0), :].astype(BF16)
            vhome[block(2), :] = vparts[block(2), :].astype(BF16)
            near_far(back2, back4, (dv1.start, dv2.start))
            for b in range(3):
                term = (first_coef * vparts[block(mine[b]), :]).astype(BF16)
                for s in range(n_sec):
                    rsend[s, b * share : (b + 1) * share, :] = term[s * share : (s + 1) * share]
            for c in es:
                c.start()
        p = packed[h]
        c = dot(p, vwin[...])
        att[:, head(h)] = c.astype(BF16)
        gh = g[:, head(h)]
        row_dot = jnp.sum(gh.astype(F32) * c, axis=1, keepdims=True)
        dp = dot(gh, vwin[...], NT)
        dscores[h] = (p.astype(F32) * (dp - row_dot)).astype(BF16)

    def key_terms(lo, hi):
        turned_sum = scale * dot(
            q_turned[...], dscores[:, :, lo * rows : hi * rows].reshape(heads * rows, (hi - lo) * rows))
        for j in range(lo, hi):
            kparts[block(j), :] = turned_sum[:, (j - lo) * rows : (j - lo + 1) * rows].T

    key_terms(0, 2)
    khome[block(1), :] = kparts[block(1), :].astype(BF16)
    dk4.start()
    key_terms(2, 4)
    khome[block(3), :] = kparts[block(3), :].astype(BF16)
    dk3.start()
    key_terms(4, 5)
    dk4.wait_recv()
    kparts[far, :] = kparts[far, :] + kpair[1].astype(F32)
    khome[block(0), :] = kparts[block(0), :].astype(BF16)
    pl.when(back4)(dk2.start)
    dk3.wait_recv()
    kparts[near, :] = kparts[near, :] + kpair[0].astype(F32)
    khome[block(2), :] = kparts[block(2), :].astype(BF16)
    pl.when(back2)(dk1.start)

    for c in es:
        c.wait_recv()
    total = rsend[me_s].astype(F32)
    for r in range(1, n_sec):
        total = total + rrecv[r].astype(F32)
    rhome[...] = total
    near_far(back2, back4, (rz1.start, rz2.start))

    near_far(on2, on4, (dv1.wait_recv, dv2.wait_recv))
    vg[...] = (own_coef * (vparts[own, :] + vback[0].astype(F32) + vback[1].astype(F32))).astype(BF16)

    for h in range(heads):
        dq[:, head(h)] = (scale * dot(dscores[h], kwin[...])).astype(BF16)

    near_far(on2, on4, (rz1.wait_recv, rz2.wait_recv))
    fg[...] = rhome[part(2), :] + rback[0] + rback[1]
    near_far(on2, on4, (dk1.wait_recv, dk2.wait_recv))
    kg[...] = (kparts[own, :] + kback[0].astype(F32) + kback[1].astype(F32)).astype(BF16)

    for c in fs + es + [k3, k4, v3, v4, dv3, dv4, dk3, dk4]:
        c.wait_send()
    near_far(on2, on4, *[(a.wait_send, b.wait_send) for a, b in ((fz1, fz2), (k1, k2), (v1, v2))])
    near_far(back2, back4, *[(a.wait_send, b.wait_send) for a, b in ((dv1, dv2), (dk1, dk2), (rz1, rz2))])


def place(*refs):
    n = (len(refs) - 1) // 2
    copies = [pltpu.make_async_copy(refs[i], refs[n + i], refs[-1].at[i]) for i in range(n)]
    for c in copies:
        c.start()
    for c in copies:
        c.wait()


def solution(mesh):
    n_sec, n_ctx = mesh.shape["section"], mesh.shape["ctx"]

    def per_device(queries, keys, values, firsts, grads, starts, mix_table, layer_index):
        rows, width = keys.shape[1], keys.shape[2]
        feats = queries.shape[2]
        heads = feats // width
        share = firsts.shape[0]
        window = (REACH + 1) * rows
        piece = 3 * share
        hbm = pl.BlockSpec(memory_space=pltpu.HBM)
        anyw = pl.BlockSpec(memory_space=pl.ANY)
        smem = pl.BlockSpec(memory_space=pltpu.SMEM)
        vmem = pl.BlockSpec(memory_space=pltpu.VMEM)
        shapes = [
            jax.ShapeDtypeStruct((rows, feats), BF16),
            jax.ShapeDtypeStruct((rows, feats), BF16),
            jax.ShapeDtypeStruct((rows, width), BF16),
            jax.ShapeDtypeStruct((rows, width), BF16),
            jax.ShapeDtypeStruct((share, width), F32),
        ]
        four = pltpu.SemaphoreType.DMA((2, 4))
        two = pltpu.SemaphoreType.DMA((2, 2))
        results = pl.pallas_call(
            functools.partial(kernel, n_sec, n_ctx, rows, width, heads),
            out_shape=[pltpu.VMEM(x.shape, x.dtype) for x in shapes],
            in_specs=[hbm] * 7 + [smem],
            out_specs=[vmem] * 5,
            scratch_shapes=[
                pltpu.VMEM((rows, feats), BF16),
                pltpu.VMEM((rows, feats), BF16),
                pltpu.VMEM((window, width), BF16),
                pltpu.VMEM((window, width), BF16),
                pltpu.VMEM((window, width), BF16),
                pltpu.VMEM((piece, width), BF16),
                pltpu.VMEM((n_sec, piece, width), BF16),
                pltpu.VMEM((1, rows), jnp.int32),
                pltpu.VMEM(mix_table.shape, F32),
                pltpu.VMEM((heads, rows, window), BF16),
                pltpu.VMEM((heads, rows, window), BF16),
                pltpu.VMEM((rows, window), F32),
                pltpu.VMEM((width, feats), BF16),
                pltpu.VMEM((width, feats), BF16),
                pltpu.VMEM((heads, rows, 2 * rows), F32),
                pltpu.VMEM((heads, rows, width), F32),
                pltpu.VMEM((heads, rows, width), F32),
                pltpu.VMEM((window, width), F32),
                pltpu.VMEM((window, width), F32),
                pltpu.VMEM((REACH * rows, width), BF16),
                pltpu.VMEM((REACH * rows, width), BF16),
                pltpu.VMEM((2, rows, width), BF16),
                pltpu.VMEM((2, rows, width), BF16),
                pltpu.VMEM((2, rows, width), BF16),
                pltpu.VMEM((2, rows, width), BF16),
                pltpu.VMEM((n_sec, piece, width), BF16),
                pltpu.VMEM((n_sec, piece, width), BF16),
                pltpu.VMEM((piece, width), F32),
                pltpu.VMEM((2, share, width), F32),
                pltpu.SemaphoreType.DMA((7,)),
                four,
                four,
                two,
                pltpu.SemaphoreType.DMA((2, n_sec)),
                four,
                four,
                pltpu.SemaphoreType.DMA((2, n_sec)),
                two,
            ],
            compiler_params=pltpu.CompilerParams(
                collective_id=0, has_side_effects=True, vmem_limit_bytes=48 << 20),
            cost_estimate=pl.CostEstimate(
                flops=12 * rows * feats * window, bytes_accessed=8 * rows * feats,
                transcendentals=rows * heads * window),
            name="attention",
        )(*[
            pltpu.with_memory_space_constraint(x, pltpu.HBM)
            for x in (queries[0], keys[0], values[0], firsts, grads[0], starts.reshape(1, rows), mix_table)
        ], layer_index)
        att, dq, kg, vg, fg = pl.pallas_call(
            place,
            out_shape=shapes,
            in_specs=[anyw] * 5,
            out_specs=[hbm] * 5,
            scratch_shapes=[pltpu.SemaphoreType.DMA((5,))],
            compiler_params=pltpu.CompilerParams(vmem_limit_bytes=8 << 20),
            name="place",
        )(*results)
        return att[None], dq[None], kg[None], vg[None], fg

    return jax.shard_map(
        per_device,
        mesh=mesh,
        in_specs=(
            P("section", "ctx", None),
            P("section", "ctx", None),
            P("section", "ctx", None),
            P(("ctx", "section"), None),
            P("section", "ctx", None),
            P("ctx"),
            P(),
            P("section"),
        ),
        out_specs=(
            P("section", "ctx", None),
            P("section", "ctx", None),
            P("section", "ctx", None),
            P("section", "ctx", None),
            P(("ctx", "section"), None),
        ),
        check_vma=False,
    )
```

```python
import functools
import math

import jax
import jax.numpy as jnp
from jax import lax
from jax.experimental import pallas as pl
from jax.experimental.pallas import tpu as pltpu
from jax.sharding import PartitionSpec as P

REACH = 4
BF16 = jnp.bfloat16
F32 = jnp.float32
NN = (((1,), (0,)), ((), ()))
NT = (((1,), (1,)), ((), ()))


def dot(a, b, dims=NN):
    return lax.dot_general(a, b, dims, preferred_element_type=F32)


def kernel(
    n_sec, n_ctx, rows, width, heads,
    q_hbm, k_hbm, v_hbm, f_hbm, g_hbm, start_hbm, mix_hbm, layer_ref,
    att, dq, kg, vg, fg,
    q, g, kwin, vwin, vraw, fpart, fall, starts, mix, packed, dscores, bias,
    q_turned, g_turned, early, early_top, early_sum,
    vparts, kparts, vhome, khome, vpair, kpair, vback, kback, rsend, rrecv, rhome, rback,
    loc, ksem, vsem, fzsem, fssem, dvsem, dksem, essem, rzsem,
):
    me_s = lax.axis_index("section")
    me_c = lax.axis_index("ctx")
    odd = lax.rem(me_c, 2)
    scale = 1.0 / math.sqrt(width)
    share = rows // n_sec
    mine = (0, 2, 4)

    def block(j):
        return pl.ds(j * rows, rows)

    def part(b):
        return pl.ds(b * share, share)

    def head(h):
        return pl.ds(h * width, width)

    def at_sec(r):
        return {"section": lax.rem(me_s + r, n_sec), "ctx": me_c}

    def at_ctx(o):
        return {"section": me_s, "ctx": me_c + o}

    mate = {"section": me_s, "ctx": me_c + 1 - 2 * odd}
    own = block(REACH)
    near = pl.ds((4 - 2 * odd) * rows, rows)
    far = pl.ds((2 - 2 * odd) * rows, rows)

    def remote(src, dst, sems, i, device):
        return pltpu.make_async_remote_copy(src, dst, sems.at[0, i], sems.at[1, i], device_id=device)

    loads = [
        pltpu.make_async_copy(a, b, loc.at[i])
        for i, (a, b) in enumerate([
            (k_hbm, kwin.at[own]),
            (f_hbm, fpart.at[part(2)]),
            (v_hbm, vraw.at[own]),
            (start_hbm, starts),
            (mix_hbm, mix),
            (q_hbm, q),
            (g_hbm, g),
        ])
    ]
    in_k, in_f, in_v, in_start, in_mix, in_q, in_g = loads

    back2, back4 = me_c >= 2, me_c >= 4
    on2, on4 = me_c + 2 < n_ctx, me_c + 4 < n_ctx

    barrier = pltpu.get_barrier_semaphore()
    for there, o in ((on4, 4), (on2, 2), (back2, -2), (back4, -4)):
        @pl.when(there)
        def _():
            pl.semaphore_signal(barrier, inc=1, device_id=at_ctx(o))
    pl.semaphore_signal(barrier, inc=1, device_id=mate)
    for r in range(1, n_sec):
        pl.semaphore_signal(barrier, inc=1, device_id=at_sec(r))
    for c in loads:
        c.start()

    fz1 = remote(f_hbm, fpart.at[part(1)], fzsem, 0, at_ctx(2))
    fz2 = remote(f_hbm, fpart.at[part(0)], fzsem, 1, at_ctx(4))
    fs = [remote(fpart, fall.at[me_s], fssem, r, at_sec(r)) for r in range(1, n_sec)]
    k1 = remote(k_hbm, kwin.at[block(2)], ksem, 0, at_ctx(2))
    k2 = remote(k_hbm, kwin.at[block(0)], ksem, 1, at_ctx(4))
    k3 = remote(kwin.at[near], kwin.at[block(3)], ksem, 2, mate)
    k4 = remote(kwin.at[far], kwin.at[block(1)], ksem, 3, mate)
    v1 = remote(v_hbm, vraw.at[block(2)], vsem, 0, at_ctx(2))
    v2 = remote(v_hbm, vraw.at[block(0)], vsem, 1, at_ctx(4))
    v3 = remote(vwin.at[near], vwin.at[block(3)], vsem, 2, mate)
    v4 = remote(vwin.at[far], vwin.at[block(1)], vsem, 3, mate)
    dv1 = remote(vhome.at[block(2)], vback.at[0], dvsem, 0, at_ctx(-2))
    dv2 = remote(vhome.at[block(0)], vback.at[1], dvsem, 1, at_ctx(-4))
    dv3 = remote(vhome.at[block(3)], vpair.at[0], dvsem, 2, mate)
    dv4 = remote(vhome.at[block(1)], vpair.at[1], dvsem, 3, mate)
    dk1 = remote(khome.at[block(2)], kback.at[0], dksem, 0, at_ctx(-2))
    dk2 = remote(khome.at[block(0)], kback.at[1], dksem, 1, at_ctx(-4))
    dk3 = remote(khome.at[block(3)], kpair.at[0], dksem, 2, mate)
    dk4 = remote(khome.at[block(1)], kpair.at[1], dksem, 3, mate)
    es = [remote(rsend.at[lax.rem(me_s + r, n_sec)], rrecv.at[r], essem, r, at_sec(r)) for r in range(1, n_sec)]
    rz1 = remote(rhome.at[part(1)], rback.at[0], rzsem, 0, at_ctx(-2))
    rz2 = remote(rhome.at[part(0)], rback.at[1], rzsem, 1, at_ctx(-4))

    @pl.when(jnp.logical_not(back4))
    def _():
        for ref, size in ((kwin, rows), (vraw, rows), (fpart, share)):
            ref[pl.ds(0, size), :] = jnp.zeros((size, width), BF16)

    @pl.when(jnp.logical_not(back2))
    def _():
        for ref, lo, size in ((kwin, 2 * rows, rows), (vraw, 2 * rows, rows), (fpart, share, share)):
            ref[pl.ds(lo, size), :] = jnp.zeros((size, width), BF16)

    for there, i in ((on2, 0), (on4, 1)):
        @pl.when(jnp.logical_not(there))
        def _():
            for ref in (vback, kback, rback):
                ref[i] = jnp.zeros(ref.shape[1:], ref.dtype)

    def near_far(there2, there4, *actions):
        for act2, act4 in actions:
            pl.when(there4)(act4)
            pl.when(there2)(act2)

    in_q.wait()
    for h in range(heads):
        q_turned[:, head(h)] = q[:, head(h)].T
    in_g.wait()
    for h in range(heads):
        g_turned[:, head(h)] = g[:, head(h)].T
    ahead = lax.convert_element_type(on2, jnp.int32) + lax.convert_element_type(on4, jnp.int32)
    behind = lax.convert_element_type(back2, jnp.int32) + lax.convert_element_type(back4, jnp.int32)
    pl.semaphore_wait(barrier, n_sec + ahead + behind)
    near_far(on2, on4, (fz1.start, fz2.start), (k1.start, k2.start))
    in_k.wait()

    @pl.when(odd == 0)
    def _():
        k3.start()

    in_start.wait()
    window = (REACH + 1) * rows
    key_at = (me_c - REACH) * rows + lax.broadcasted_iota(jnp.int32, (window, rows), 0)
    query_at = me_c * rows + lax.broadcasted_iota(jnp.int32, (window, rows), 1)
    turned = jnp.where((key_at >= starts[...]) & (key_at <= query_at), 0.0, -jnp.inf).astype(F32)
    for j in range(REACH + 1):
        bias[:, block(j)] = turned[j * rows : (j + 1) * rows].T

    in_mix.wait()
    coeffs = mix[pl.ds(layer_ref[0], 1), :]
    own_coef = coeffs[:, :width]
    first_coef = coeffs[:, width:]

    in_f.wait()

    @pl.when(back2)
    def _():
        k1.wait_recv()

    @pl.when(odd == 0)
    def _():
        k4.start()

    @pl.when(odd == 1)
    def _():
        k3.start()

    near_far(on2, on4, (v1.start, v2.start))
    near_far(back2, back4, (fz1.wait_recv, fz2.wait_recv))
    for c in fs:
        c.start()
    for h in range(heads):
        if h == heads // 2:
            pl.when(back4)(k2.wait_recv)
            pl.when(odd == 1)(k4.start)
        qh = q[:, head(h)]
        s4 = dot(qh, kwin[block(4), :], NT) + bias[:, block(4)]
        s2 = dot(qh, kwin[block(2), :], NT) + bias[:, block(2)]
        top = jnp.max(jnp.maximum(s4, s2), axis=1, keepdims=True)
        e4 = jnp.exp((s4 - top) * scale)
        e2 = jnp.exp((s2 - top) * scale)
        early[h, :, :rows] = e2
        early[h, :, rows:] = e4
        early_top[h] = jnp.broadcast_to(top, (rows, width))
        early_sum[h] = jnp.broadcast_to(jnp.sum(e4 + e2, axis=1, keepdims=True), (rows, width))

    k3.wait_recv()
    k4.wait_recv()
    for h in range(heads):
        qh = q[:, head(h)]
        s0 = dot(qh, kwin[pl.ds(0, 2 * rows), :], NT) + bias[:, : 2 * rows]
        s3 = dot(qh, kwin[block(3), :], NT) + bias[:, block(3)]
        late_top = jnp.max(jnp.maximum(jnp.maximum(s0[:, :rows], s0[:, rows:]), s3), axis=1, keepdims=True)
        top = jnp.maximum(early_top[h], late_top)
        e0 = jnp.exp((s0[:, :rows] - top) * scale)
        e1 = jnp.exp((s0[:, rows:] - top) * scale)
        e3 = jnp.exp((s3 - top) * scale)
        fade = jnp.exp((early_top[h] - top) * scale)
        inverse = 1.0 / (jnp.sum(e0 + e1 + e3, axis=1, keepdims=True) + early_sum[h] * fade)
        fade = fade * inverse
        packed[h, :, block(0)] = (e0 * inverse).astype(BF16)
        packed[h, :, block(1)] = (e1 * inverse).astype(BF16)
        packed[h, :, block(2)] = (early[h, :, :rows] * fade).astype(BF16)
        packed[h, :, block(3)] = (e3 * inverse).astype(BF16)
        packed[h, :, block(4)] = (early[h, :, rows:] * fade).astype(BF16)

    in_v.wait()
    near_far(back2, back4, (v1.wait_recv, v2.wait_recv))
    fall[me_s] = fpart[...]
    for c in fs:
        c.wait_recv()
    for b in (2, 1, 0):
        firsts = jnp.concatenate([fall[s, b * share : (b + 1) * share, :] for s in range(n_sec)], axis=0)
        vwin[block(mine[b]), :] = (
            own_coef * vraw[block(mine[b]), :].astype(F32) + first_coef * firsts.astype(F32)
        ).astype(BF16)
    v3.start()
    v4.start()

    for lo, hi in ((0, 2), (2, 4), (4, 5)):
        turned_sum = dot(g_turned[...], packed[:, :, lo * rows : hi * rows].reshape(heads * rows, (hi - lo) * rows))
        for j in range(lo, hi):
            vparts[block(j), :] = turned_sum[:, (j - lo) * rows : (j - lo + 1) * rows].T
        if lo == 0:
            vhome[block(1), :] = vparts[block(1), :].astype(BF16)
            dv4.start()

            @pl.when(odd == 0)
            def _():
                vhome[block(0), :] = vparts[block(0), :].astype(BF16)
                pl.when(back4)(dv2.start)
        if lo == 2:
            vhome[block(3), :] = vparts[block(3), :].astype(BF16)
            dv3.start()
    v3.wait_recv()
    v4.wait_recv()

    for h in range(heads):
        if h == heads // 4:
            dv4.wait_recv()
            dv3.wait_recv()
            vparts[far, :] = vparts[far, :] + vpair[1].astype(F32)
            vparts[near, :] = vparts[near, :] + vpair[0].astype(F32)

            @pl.when(odd == 1)
            def _():
                vhome[block(0), :] = vparts[block(0), :].astype(BF16)
                pl.when(back4)(dv2.start)

            vhome[block(2), :] = vparts[block(2), :].astype(BF16)
            pl.when(back2)(dv1.start)
            for b in range(3):
                term = (first_coef * vparts[block(mine[b]), :]).astype(BF16)
                for s in range(n_sec):
                    rsend[s, b * share : (b + 1) * share, :] = term[s * share : (s + 1) * share]
            for c in es:
                c.start()
        p = packed[h]
        c = dot(p, vwin[...])
        att[:, head(h)] = c.astype(BF16)
        gh = g[:, head(h)]
        row_dot = jnp.sum(gh.astype(F32) * c, axis=1, keepdims=True)
        dp = dot(gh, vwin[...], NT)
        dscores[h] = (p.astype(F32) * (dp - row_dot)).astype(BF16)

    def key_terms(lo, hi):
        turned_sum = scale * dot(
            q_turned[...], dscores[:, :, lo * rows : hi * rows].reshape(heads * rows, (hi - lo) * rows))
        for j in range(lo, hi):
            kparts[block(j), :] = turned_sum[:, (j - lo) * rows : (j - lo + 1) * rows].T

    key_terms(0, 2)
    khome[block(1), :] = kparts[block(1), :].astype(BF16)
    dk4.start()

    @pl.when(odd == 0)
    def _():
        khome[block(0), :] = kparts[block(0), :].astype(BF16)
        pl.when(back4)(dk2.start)

    key_terms(2, 4)
    khome[block(3), :] = kparts[block(3), :].astype(BF16)
    dk3.start()
    key_terms(4, 5)
    dk4.wait_recv()
    kparts[far, :] = kparts[far, :] + kpair[1].astype(F32)

    @pl.when(odd == 1)
    def _():
        khome[block(0), :] = kparts[block(0), :].astype(BF16)
        pl.when(back4)(dk2.start)

    dk3.wait_recv()
    kparts[near, :] = kparts[near, :] + kpair[0].astype(F32)
    khome[block(2), :] = kparts[block(2), :].astype(BF16)
    pl.when(back2)(dk1.start)

    for c in es:
        c.wait_recv()
    total = rsend[me_s].astype(F32)
    for r in range(1, n_sec):
        total = total + rrecv[r].astype(F32)
    rhome[...] = total
    near_far(back2, back4, (rz1.start, rz2.start))

    near_far(on2, on4, (dv1.wait_recv, dv2.wait_recv))
    vg[...] = (own_coef * (vparts[own, :] + vback[0].astype(F32) + vback[1].astype(F32))).astype(BF16)

    for h in range(heads):
        dq[:, head(h)] = (scale * dot(dscores[h], kwin[...])).astype(BF16)

    near_far(on2, on4, (rz1.wait_recv, rz2.wait_recv))
    fg[...] = rhome[part(2), :] + rback[0] + rback[1]
    near_far(on2, on4, (dk1.wait_recv, dk2.wait_recv))
    kg[...] = (kparts[own, :] + kback[0].astype(F32) + kback[1].astype(F32)).astype(BF16)

    for c in fs + es + [k3, k4, v3, v4, dv3, dv4, dk3, dk4]:
        c.wait_send()
    near_far(on2, on4, *[(a.wait_send, b.wait_send) for a, b in ((fz1, fz2), (k1, k2), (v1, v2))])
    near_far(back2, back4, *[(a.wait_send, b.wait_send) for a, b in ((dv1, dv2), (dk1, dk2), (rz1, rz2))])


def place(*refs):
    n = (len(refs) - 1) // 2
    copies = [pltpu.make_async_copy(refs[i], refs[n + i], refs[-1].at[i]) for i in range(n)]
    for c in copies:
        c.start()
    for c in copies:
        c.wait()


def solution(mesh):
    n_sec, n_ctx = mesh.shape["section"], mesh.shape["ctx"]

    def per_device(queries, keys, values, firsts, grads, starts, mix_table, layer_index):
        rows, width = keys.shape[1], keys.shape[2]
        feats = queries.shape[2]
        heads = feats // width
        share = firsts.shape[0]
        window = (REACH + 1) * rows
        piece = 3 * share
        hbm = pl.BlockSpec(memory_space=pltpu.HBM)
        anyw = pl.BlockSpec(memory_space=pl.ANY)
        smem = pl.BlockSpec(memory_space=pltpu.SMEM)
        vmem = pl.BlockSpec(memory_space=pltpu.VMEM)
        shapes = [
            jax.ShapeDtypeStruct((rows, feats), BF16),
            jax.ShapeDtypeStruct((rows, feats), BF16),
            jax.ShapeDtypeStruct((rows, width), BF16),
            jax.ShapeDtypeStruct((rows, width), BF16),
            jax.ShapeDtypeStruct((share, width), F32),
        ]
        four = pltpu.SemaphoreType.DMA((2, 4))
        two = pltpu.SemaphoreType.DMA((2, 2))
        results = pl.pallas_call(
            functools.partial(kernel, n_sec, n_ctx, rows, width, heads),
            out_shape=[pltpu.VMEM(x.shape, x.dtype) for x in shapes],
            in_specs=[hbm] * 7 + [smem],
            out_specs=[vmem] * 5,
            scratch_shapes=[
                pltpu.VMEM((rows, feats), BF16),
                pltpu.VMEM((rows, feats), BF16),
                pltpu.VMEM((window, width), BF16),
                pltpu.VMEM((window, width), BF16),
                pltpu.VMEM((window, width), BF16),
                pltpu.VMEM((piece, width), BF16),
                pltpu.VMEM((n_sec, piece, width), BF16),
                pltpu.VMEM((1, rows), jnp.int32),
                pltpu.VMEM(mix_table.shape, F32),
                pltpu.VMEM((heads, rows, window), BF16),
                pltpu.VMEM((heads, rows, window), BF16),
                pltpu.VMEM((rows, window), F32),
                pltpu.VMEM((width, feats), BF16),
                pltpu.VMEM((width, feats), BF16),
                pltpu.VMEM((heads, rows, 2 * rows), F32),
                pltpu.VMEM((heads, rows, width), F32),
                pltpu.VMEM((heads, rows, width), F32),
                pltpu.VMEM((window, width), F32),
                pltpu.VMEM((window, width), F32),
                pltpu.VMEM((REACH * rows, width), BF16),
                pltpu.VMEM((REACH * rows, width), BF16),
                pltpu.VMEM((2, rows, width), BF16),
                pltpu.VMEM((2, rows, width), BF16),
                pltpu.VMEM((2, rows, width), BF16),
                pltpu.VMEM((2, rows, width), BF16),
                pltpu.VMEM((n_sec, piece, width), BF16),
                pltpu.VMEM((n_sec, piece, width), BF16),
                pltpu.VMEM((piece, width), F32),
                pltpu.VMEM((2, share, width), F32),
                pltpu.SemaphoreType.DMA((7,)),
                four,
                four,
                two,
                pltpu.SemaphoreType.DMA((2, n_sec)),
                four,
                four,
                pltpu.SemaphoreType.DMA((2, n_sec)),
                two,
            ],
            compiler_params=pltpu.CompilerParams(
                collective_id=0, has_side_effects=True, vmem_limit_bytes=48 << 20),
            cost_estimate=pl.CostEstimate(
                flops=12 * rows * feats * window, bytes_accessed=8 * rows * feats,
                transcendentals=rows * heads * window),
            name="attention",
        )(*[
            pltpu.with_memory_space_constraint(x, pltpu.HBM)
            for x in (queries[0], keys[0], values[0], firsts, grads[0], starts.reshape(1, rows), mix_table)
        ], layer_index)
        att, dq, kg, vg, fg = pl.pallas_call(
            place,
            out_shape=shapes,
            in_specs=[anyw] * 5,
            out_specs=[hbm] * 5,
            scratch_shapes=[pltpu.SemaphoreType.DMA((5,))],
            compiler_params=pltpu.CompilerParams(vmem_limit_bytes=8 << 20),
            name="place",
        )(*results)
        return att[None], dq[None], kg[None], vg[None], fg

    return jax.shard_map(
        per_device,
        mesh=mesh,
        in_specs=(
            P("section", "ctx", None),
            P("section", "ctx", None),
            P("section", "ctx", None),
            P(("ctx", "section"), None),
            P("section", "ctx", None),
            P("ctx"),
            P(),
            P("section"),
        ),
        out_specs=(
            P("section", "ctx", None),
            P("section", "ctx", None),
            P("section", "ctx", None),
            P("section", "ctx", None),
            P(("ctx", "section"), None),
        ),
        check_vma=False,
    )
```
